256 devices in a mesh: grp: 32 (over z_hi, x, y), tp: 8 (over z_lo, core).
Axes of the slice: x: 4, y: 4, z: 8 (z_hi: 2, z_lo: 4; z = z_hi * 4 + z_lo), core: 2. Of those that a mesh axis runs over, the one named last changes fastest.
Arguments:
- queries: bfloat16 [3, 32, 24, 4096], P(None, 'grp', None, 'tp'), may hold values from -12 to 12
- fresh_pairs: bfloat16 [3, 32, 24, 2, 1024], P(None, 'grp', None, None, 'tp'), may hold values from -6 to 6
- cache_pool: bfloat16 [32, 80, 2, 128, 1024], P('grp', None, None, None, 'tp'), may hold values from -6 to 6
- out_weight: bfloat16 [4096, 4096], P('tp'), may hold values from -0.8984375 to 0.8984375
- lengths: int32 [32, 24], P('grp'), may hold values from 1 to 509, as said below
- page_table: int32 [32, 24, 4], P('grp'), may hold values from 0 to 79, as said below
- victims: int32 [32, 16], P('grp'), may hold values from 0 to 23, as said below
- victim_dest: int32 [32, 16], replicated, may hold values from 0 to 31, as said below
- section_plan: int32 [32, 16, 3], replicated, may hold values from 0 to 2, as said below
Outputs:
- projected: bfloat16 [32, 24, 3, 4096], P('grp', 'tp')
- migrated: bfloat16 [32, 16, 3, 2, 128, 1024], P('grp', None, None, None, None, 'tp')
The draws below stay inside these ranges and needn't reach their ends.
Inputs may be any that keep to these rules, and one draw needn't show every extreme that they name: `lengths`: in every group each victim holds between 256 and 381 tokens, and one other request holds exactly 509. `page_table`: the first ceil((lengths + 3) / 128) entries of a request are pool pages that no other request of the group names among its first entries; later entries are unused. `victims`: 16 distinct requests of the group. `victim_dest`: A group's victims go to 16 distinct groups other than itself; for each j, every group is the target of victim j of exactly one source. `section_plan`: for each victim, a permutation of its pages 0 .. 3 - 1 over the steps.
All inputs are finite; a program needn't handle non-finite values.
Results may differ from the reference program's by a relative error of at most 0.0051.
Values may be sent and summed in bfloat16 or wider, within the bound.
No kernel may reach another device: no remote copies, remote signals or barrier semaphores. Data moves between devices by JAX's collectives and lax.ppermute only.
A program may use at most 128 MiB of HBM per device.

```python
import math
import jax
import jax.numpy as jnp
from jax import lax

D = 4096
QUERY_HEAD_COUNT = 32
KEY_VALUE_HEADS = 8
HEAD_SIZE = 128
PAGE_TOKENS = 128
DECODE_STEPS = 3
GROUP_REQUESTS = 24
PMAX = 4
MOVING_REQUESTS = 16
SERVING_GROUPS = 32
POOL_PAGES = 80
VLO = 256
VHI = 381
LONGEST = 509


def shuffle_rows(base, count, size):

    def shuffle_one(entry_key):
        return jax.random.permutation(entry_key, size)
    return jax.vmap(shuffle_one)(jax.random.split(base, count)).astype(jnp.int32)


def plan_tables(key):
    streams = jax.random.split(key, 7)
    order = shuffle_rows(streams[0], SERVING_GROUPS, GROUP_REQUESTS)
    chosen = order[:, :MOVING_REQUESTS]
    longest = order[:, MOVING_REQUESTS]
    picked = (chosen[:, :, None] == jnp.arange(GROUP_REQUESTS)[None, None, :]).astype(jnp.int32)
    victim_len = jax.random.randint(streams[1], (SERVING_GROUPS, MOVING_REQUESTS), VLO, VHI + 1)
    other_len = jax.random.randint(streams[2], (SERVING_GROUPS, GROUP_REQUESTS), 1, LONGEST + 1)
    is_victim = jnp.sum(picked, axis=1)
    lengths = jnp.where(is_victim > 0, jnp.sum(picked * victim_len[:, :, None], axis=1), other_len)
    lengths = jnp.where(jnp.arange(GROUP_REQUESTS)[None, :] == longest[:, None], LONGEST, lengths)
    pages = (lengths + DECODE_STEPS + PAGE_TOKENS - 1) // PAGE_TOKENS
    starts = jnp.cumsum(pages, axis=1) - pages
    shuffled = shuffle_rows(streams[3], SERVING_GROUPS, POOL_PAGES)
    spots = (starts[:, :, None] + jnp.arange(PMAX)[None, None, :]) % POOL_PAGES
    table = jnp.take_along_axis(shuffled, spots.reshape(SERVING_GROUPS, GROUP_REQUESTS * PMAX), axis=1).reshape(SERVING_GROUPS, GROUP_REQUESTS, PMAX)
    sigma = jax.random.permutation(streams[4], SERVING_GROUPS).astype(jnp.int32)
    inverse = jnp.argsort(sigma).astype(jnp.int32)
    offsets = 1 + jax.random.permutation(streams[5], SERVING_GROUPS - 1)[:MOVING_REQUESTS].astype(jnp.int32)
    dest = sigma[(inverse[:, None] + offsets[None, :]) % SERVING_GROUPS]
    ranks = jax.random.randint(streams[6], (SERVING_GROUPS, MOVING_REQUESTS, DECODE_STEPS), 0, 1000) * DECODE_STEPS + jnp.arange(DECODE_STEPS)
    plan = jnp.argsort(ranks, axis=-1).astype(jnp.int32)
    return (lengths.astype(jnp.int32), table.astype(jnp.int32), chosen, dest.astype(jnp.int32), plan)


def fresh_normal(key):
    return jnp.clip(jax.random.normal(key, (DECODE_STEPS, SERVING_GROUPS, GROUP_REQUESTS, 2, KEY_VALUE_HEADS * HEAD_SIZE)), -6.0, 6.0)


def spread_heads(token_rows):
    array_shape = token_rows.shape[:-1]
    section_split = token_rows.reshape(array_shape + (KEY_VALUE_HEADS, 1, HEAD_SIZE))
    return jnp.broadcast_to(section_split, array_shape + (KEY_VALUE_HEADS, QUERY_HEAD_COUNT // KEY_VALUE_HEADS, HEAD_SIZE)).reshape(array_shape + (QUERY_HEAD_COUNT * HEAD_SIZE,))


def draw_lengths(key, part):
    tables = plan_tables(key)
    return tables[0]


def draw_page_table(key, part):
    tables = plan_tables(key)
    return tables[1]


def draw_victims(key, part):
    tables = plan_tables(key)
    return tables[2]


def draw_victim_dest(key, part):
    tables = plan_tables(key)
    return tables[3]


def draw_section_plan(key, part):
    tables = plan_tables(key)
    return tables[4]


def draw_fresh_pairs(key, part):
    base = fresh_normal(key)
    return base.astype(jnp.bfloat16)


def draw_queries(key, part):
    base = fresh_normal(key)
    key = jax.random.fold_in(key, 3)
    own_keys = spread_heads(base[:, :, :, 0, :])
    noise = jnp.clip(jax.random.normal(key, own_keys.shape), -6.0, 6.0)
    value_rows = 0.4 * own_keys + noise
    return jnp.clip(value_rows, -12.0, 12.0).astype(jnp.bfloat16)


def draw_cache_pool(key, part):
    key = jax.random.fold_in(key, 5)
    value_rows = jnp.clip(jax.random.normal(key, (SERVING_GROUPS, POOL_PAGES, 2, PAGE_TOKENS, KEY_VALUE_HEADS * HEAD_SIZE)), -6.0, 6.0)
    return value_rows.astype(jnp.bfloat16)


def spiked(array, key, source, target, shards_of, factor):
    def block_of(position):
        return (jnp.arange(array.shape[position]) // (array.shape[position] // shards_of)).reshape((-1,) + (1,) * (array.ndim - 1 - position))

    one_side = jax.random.permutation(key, shards_of)[block_of(target)]
    second = (block_of(target) + shards_of // 2) % shards_of
    return jnp.where((block_of(source) == one_side) | (block_of(source) == second), factor * array, array)


def shard_levels(key, extent, shards, least, high):
    factor_of = 1.0
    for dim, blocks in shards:
        steps = jax.random.uniform(jax.random.fold_in(jax.random.fold_in(key, 6), dim), (blocks,), jnp.float32, least / len(shards), high / len(shards))
        factor_of = factor_of * jnp.repeat(jnp.exp(steps), extent[dim] // blocks).reshape((-1,) + (1,) * (len(extent) - 1 - dim))
    return factor_of


def bell_draw_with(own_key, extent, width, bound, cuts, heavy, kind=jnp.bfloat16):
    result = width * jax.random.normal(own_key, extent, jnp.float32)
    if cuts:
        result = result * shard_levels(own_key, extent, cuts, -0.22, 0.18)
    return jnp.clip(spiked(result, jax.random.fold_in(own_key, 3), *heavy), -bound, bound).astype(kind)


def setup_inputs(seed: int = 0) -> dict:
    splits = jax.random.split(jax.random.key(seed), 10)
    return {
        "queries": draw_queries(jax.random.fold_in(splits[9], 71), 0),
        "fresh_pairs": draw_fresh_pairs(jax.random.fold_in(splits[9], 71), 0),
        "cache_pool": draw_cache_pool(jax.random.fold_in(splits[9], 71), 0),
        "out_weight": bell_draw_with(splits[3], (QUERY_HEAD_COUNT * HEAD_SIZE, D), 0.15, 0.8984375, ((0, 8),), (0, 1, 8, 2.0)),
        "lengths": draw_lengths(jax.random.fold_in(splits[9], 71), 0),
        "page_table": draw_page_table(jax.random.fold_in(splits[9], 71), 0),
        "victims": draw_victims(jax.random.fold_in(splits[9], 71), 0),
        "victim_dest": draw_victim_dest(jax.random.fold_in(splits[9], 71), 0),
        "section_plan": draw_section_plan(jax.random.fold_in(splits[9], 71), 0),
    }


masked_score = -1e+30

def attend(query_matrix, cache, table, positions):
    request_list = table.shape[0]
    section_span = PMAX * PAGE_TOKENS
    gathered_pages = cache[table]
    key_rows = gathered_pages[:, :, 0].reshape(request_list, section_span, KEY_VALUE_HEADS, HEAD_SIZE).astype(jnp.float32)
    value_rows = gathered_pages[:, :, 1].reshape(request_list, section_span, KEY_VALUE_HEADS, HEAD_SIZE).astype(jnp.float32)
    grouped_heads = query_matrix.reshape(request_list, KEY_VALUE_HEADS, QUERY_HEAD_COUNT // KEY_VALUE_HEADS, HEAD_SIZE).astype(jnp.float32)
    scores = jnp.einsum('rhgd,rkhd->rhgk', grouped_heads, key_rows) / math.sqrt(HEAD_SIZE)
    visible = jnp.arange(section_span)[None, :] <= positions[:, None]
    scores = jnp.where(visible[:, None, None, :], scores, masked_score)
    peak = lax.optimization_barrier(jnp.max(scores, axis=-1, keepdims=True))
    weights = jnp.exp(scores - peak)
    total = lax.optimization_barrier(jnp.sum(weights, axis=-1, keepdims=True))
    probs = lax.optimization_barrier(weights.astype(jnp.bfloat16)).astype(jnp.float32)
    summed = jnp.einsum('rhgk,rkhd->rhgd', probs, value_rows)
    return (summed / total).astype(jnp.bfloat16).reshape(request_list, QUERY_HEAD_COUNT * HEAD_SIZE)

def group_decode(items):
    query_block, fresh_block, cache, table, request_lengths, chosen, plan = items
    token_rows = jnp.arange(GROUP_REQUESTS)
    slots = jnp.arange(MOVING_REQUESTS)
    victim_pages = table[chosen][:, :DECODE_STEPS]
    sent_pages = jnp.zeros((MOVING_REQUESTS, DECODE_STEPS, 2, PAGE_TOKENS, KEY_VALUE_HEADS * HEAD_SIZE), jnp.bfloat16)
    attended = []
    for section_index in range(DECODE_STEPS):
        positions = request_lengths + section_index
        cache = cache.at[table[token_rows, positions // PAGE_TOKENS], :, positions % PAGE_TOKENS].set(fresh_block[section_index])
        attended.append(attend(query_block[section_index], cache, table, positions))
        picked = plan[:, section_index]
        content = cache[victim_pages[slots, picked]]
        sent_pages = sent_pages.at[slots, picked].set(content)
    return (jnp.stack(attended, axis=1), sent_pages)

def reference(queries, fresh_pairs, cache_pool, out_weight, lengths, page_table, victims, victim_dest, section_plan):
    attended, sent_pages = lax.map(group_decode, (jnp.moveaxis(queries, 1, 0), jnp.moveaxis(fresh_pairs, 1, 0), cache_pool, page_table, lengths, victims, section_plan))
    flat = attended.reshape(SERVING_GROUPS * GROUP_REQUESTS * DECODE_STEPS, QUERY_HEAD_COUNT * HEAD_SIZE)
    projected = jnp.dot(flat, out_weight, preferred_element_type=jnp.float32).astype(jnp.bfloat16)
    projected = projected.reshape(SERVING_GROUPS, GROUP_REQUESTS, DECODE_STEPS, D)
    slots = jnp.arange(MOVING_REQUESTS, dtype=jnp.int32)
    source = jnp.zeros((SERVING_GROUPS, MOVING_REQUESTS), jnp.int32).at[victim_dest, slots[None, :]].set(jnp.arange(SERVING_GROUPS, dtype=jnp.int32)[:, None])
    migrated = sent_pages[source, slots[None, :]]
    return (projected, migrated)
```

```python
import math

import jax
import jax.numpy as jnp
from jax import lax
from jax.experimental import pallas as pl
from jax.experimental.pallas import tpu as pltpu
from jax.sharding import PartitionSpec as P

HEAD_SIZE = 128
HALVES = 2
STRAIGHT = 8
LIFTED = 2


masked_score = -1e30


def attend_all(query_steps, fresh_steps, cache, table, request_lengths, kv_heads, query_heads):
    steps_total, request_list = (query_steps.shape[0], query_steps.shape[1])
    entries = table.shape[1]
    section_span = entries * cache.shape[2]
    key_rows = cache[table, 0].reshape(request_list, section_span, kv_heads, HEAD_SIZE)
    value_rows = cache[table, 1].reshape(request_list, section_span, kv_heads, HEAD_SIZE)
    grouped_heads = query_steps.reshape(
        steps_total, request_list, kv_heads, query_heads // kv_heads, HEAD_SIZE
    )
    fresh_keys = fresh_steps[:, :, 0].reshape(steps_total, request_list, kv_heads, HEAD_SIZE)
    fresh_values = fresh_steps[:, :, 1].reshape(steps_total, request_list, kv_heads, HEAD_SIZE)
    scale = math.sqrt(HEAD_SIZE)
    old_scores = (
        jnp.einsum("srhgd,rkhd->rhgsk", grouped_heads, key_rows, preferred_element_type=jnp.float32)
        / scale
    )
    new_scores = (
        jnp.einsum(
            "srhgd,trhd->rhgst", grouped_heads, fresh_keys, preferred_element_type=jnp.float32
        )
        / scale
    )
    old_visible = jnp.arange(section_span)[None, :] < request_lengths[:, None]
    old_scores = jnp.where(old_visible[:, None, None, None, :], old_scores, masked_score)
    new_visible = jnp.arange(steps_total)[None, :] <= jnp.arange(steps_total)[:, None]
    new_scores = jnp.where(new_visible[None, None, None, :, :], new_scores, masked_score)
    peak = jnp.maximum(
        jnp.max(old_scores, axis=-1, keepdims=True), jnp.max(new_scores, axis=-1, keepdims=True)
    )
    old_weights = jnp.exp(old_scores - peak)
    new_weights = jnp.exp(new_scores - peak)
    total = jnp.sum(old_weights, axis=-1) + jnp.sum(new_weights, axis=-1)
    old_probs = old_weights.astype(jnp.bfloat16)
    new_probs = new_weights.astype(jnp.bfloat16)
    summed = jnp.einsum(
        "rhgsk,rkhd->srhgd", old_probs, value_rows, preferred_element_type=jnp.float32
    )
    summed = summed + jnp.einsum(
        "rhgst,trhd->srhgd", new_probs, fresh_values, preferred_element_type=jnp.float32
    )
    total = jnp.moveaxis(total, 3, 0)[..., None]
    return (
        (summed / total)
        .astype(jnp.bfloat16)
        .reshape(steps_total, request_list, query_heads * HEAD_SIZE)
    )


def route(own_ref, cross_ref, count_ref, via_ref, half, plane, straight):
    def source(i, carry):
        s = half * plane + i

        def pick(_, state):
            free, chosen, once, twice, bad = state
            empty = free & ~once
            pool = jnp.where(empty != 0, empty, free & ~twice)
            bit = pool & -pool
            twice = twice | (once & bit)
            return free & ~bit, chosen | bit, once | bit, twice, bad | (bit == 0).astype(jnp.int32)

        once, twice, bad = carry
        free = cross_ref[s] & ~own_ref[s]
        extra = jnp.maximum(count_ref[s] - straight, 0)
        _, chosen, once, twice, bad = lax.fori_loop(
            0, extra, pick, (free, jnp.int32(0), once, twice, bad)
        )
        via_ref[s] = chosen
        return once, twice, bad

    zero = jnp.int32(0)
    return lax.fori_loop(0, plane, source, (zero, zero, zero))[2]


def goes_via(via_ref, source, place):
    return ((via_ref[source] >> place) & 1) == 1


def first_pages_kernel(
    me_ref,
    own_ref,
    cross_ref,
    count_ref,
    table_ref,
    victim_ref,
    dest_ref,
    cache_ref,
    early_ref,
    via_ref,
    held,
    in_sem,
    out_sem,
):
    count, pages = held.shape[:2]
    groups = dest_ref.shape[1]
    plane = groups // HALVES
    straight = early_ref.shape[0]
    group = me_ref[0]
    my_half = group // plane

    def page_in(j, p):
        page = table_ref[p, victim_ref[0, j]]
        return pltpu.make_async_copy(cache_ref.at[page], held.at[j, p], in_sem.at[j])

    def copy_out(j, rank):
        return pltpu.make_async_copy(held.at[j], early_ref.at[rank], out_sem)

    def visit(act):
        rank = jnp.int32(0)
        for j in range(count):
            target = dest_ref[j, group]
            leaves = ((target // plane) != my_half) & jnp.logical_not(
                goes_via(via_ref, group, target % plane)
            )
            leaves = leaves & (rank < straight)

            @pl.when(leaves)
            def _():
                act(j, rank)

            rank = rank + jnp.where(leaves, 1, 0)

    def read(j, rank):
        for p in range(pages):
            page_in(j, p).start()

    def write(j, rank):
        for p in range(pages):
            page_in(j, p).wait()
        copy_out(j, rank).start()

    bad = route(own_ref, cross_ref, count_ref, via_ref, my_half, plane, straight)
    visit(read)
    bad = bad | route(own_ref, cross_ref, count_ref, via_ref, 1 - my_half, plane, straight)
    via_ref[groups] = bad
    visit(write)
    visit(lambda j, rank: copy_out(j, rank).wait())


def first_pages(straight, me, masks, table, victims, dest, cache, pages):
    count = victims.shape[1]
    groups = dest.shape[1]
    smem = pl.BlockSpec(memory_space=pltpu.SMEM)
    anywhere = pl.BlockSpec(memory_space=pl.ANY)
    return pl.pallas_call(
        first_pages_kernel,
        out_shape=(
            jax.ShapeDtypeStruct((straight, pages) + cache.shape[1:], cache.dtype),
            jax.ShapeDtypeStruct((groups + 1,), jnp.int32),
        ),
        in_specs=[smem] * 7 + [anywhere],
        out_specs=(anywhere, smem),
        scratch_shapes=[
            pltpu.VMEM((count, pages) + cache.shape[1:], cache.dtype),
            pltpu.SemaphoreType.DMA((count,)),
            pltpu.SemaphoreType.DMA,
        ],
        name="first_pages",
    )(me, *masks, table, victims, dest, cache)


def pack_kernel(
    me_ref,
    via_ref,
    length_ref,
    table_ref,
    victim_ref,
    dest_ref,
    plan_ref,
    fresh_ref,
    cache_ref,
    _,
    own_ref,
    late_ref,
    held,
    in_sem,
    out_sem,
):
    count, pages, rows, _ = held.shape
    steps = fresh_ref.shape[0]
    page_len = rows // 2
    plane = own_ref.shape[0]
    straight = late_ref.shape[0]
    group = me_ref[0]
    my_half = group // plane

    def page_in(j, p):
        page = table_ref[p, victim_ref[0, j]]
        return pltpu.make_async_copy(cache_ref.at[page], held.at[j, p], in_sem.at[j])

    def send(j, rank, act):
        target = dest_ref[j, group]
        place = target % plane
        in_half = ((target // plane) == my_half) | goes_via(via_ref, group, place)
        leaves = jnp.logical_not(in_half) & (rank < straight)

        @pl.when(in_half)
        def _():
            act(pltpu.make_async_copy(held.at[j], own_ref.at[place], out_sem))

        @pl.when(leaves)
        def _():
            act(pltpu.make_async_copy(held.at[j, pages - 1], late_ref.at[rank], out_sem))

        return rank + jnp.where(leaves, 1, 0)

    for j in range(count):
        for p in range(pages):
            page_in(j, p).start()
    row_ids = lax.broadcasted_iota(jnp.int32, (page_len, HEAD_SIZE), 0)
    rank = jnp.int32(0)
    for j in range(count):
        for p in range(pages):
            page_in(j, p).wait()
        victim = victim_ref[0, j]
        first = length_ref[0, victim] - (pages - 1) * page_len
        last_step = jnp.int32(0)
        for s in range(steps):
            last_step = jnp.where(plan_ref[s * count + j, group] == pages - 1, s, last_step)
        for side in range(2):
            span = pl.ds(side * page_len, page_len)
            content = held[j, pages - 1, span, :].astype(jnp.float32)
            for t in range(steps):
                row = jnp.where(t <= last_step, first + t, -1)
                token = fresh_ref[t, victim].astype(jnp.float32)[side : side + 1]
                content = jnp.where(row_ids == row, token, content)
            held[j, pages - 1, span, :] = content.astype(jnp.bfloat16)
        rank = send(j, rank, lambda copy: copy.start())
    rank = jnp.int32(0)
    for j in range(count):
        rank = send(j, rank, lambda copy: copy.wait())


def pack(straight, scalars, fresh, cache, plane, early):
    count = scalars[4].shape[1]
    steps = fresh.shape[0]
    rows, width = cache.shape[1:]
    smem = pl.BlockSpec(memory_space=pltpu.SMEM)
    anywhere = pl.BlockSpec(memory_space=pl.ANY)
    return pl.pallas_call(
        pack_kernel,
        out_shape=(
            jax.ShapeDtypeStruct((plane, steps, rows, width), cache.dtype),
            jax.ShapeDtypeStruct((straight, rows, width), cache.dtype),
        ),
        in_specs=[smem] * 7 + [pl.BlockSpec(memory_space=pltpu.VMEM), anywhere, anywhere],
        out_specs=(anywhere,) * 2,
        scratch_shapes=[
            pltpu.VMEM((count, steps, rows, width), cache.dtype),
            pltpu.SemaphoreType.DMA((count,)),
            pltpu.SemaphoreType.DMA,
        ],
        name="pack_pages",
    )(*scalars, fresh, cache, early)


def relay_kernel(me_ref, via_ref, dest_ref, got_ref, slots_ref, sem):
    plane = slots_ref.shape[0]
    count = dest_ref.shape[0]
    straight = got_ref.shape[0]
    group = me_ref[0]
    my_half = group // plane
    partner = jnp.where(group < plane, group + plane, group - plane)

    def visit(act):
        rank = jnp.int32(0)
        for j in range(count):
            target = dest_ref[j, partner]
            place = target % plane
            came = ((target // plane) == my_half) & jnp.logical_not(
                goes_via(via_ref, partner, place)
            )
            came = came & (rank < straight)

            @pl.when(came)
            def _():
                act(pltpu.make_async_copy(got_ref.at[rank], slots_ref.at[place], sem))

            rank = rank + jnp.where(came, 1, 0)

    visit(lambda copy: copy.start())
    visit(lambda copy: copy.wait())


def relay(me, via, dest, got, plane):
    smem = pl.BlockSpec(memory_space=pltpu.SMEM)
    return pl.pallas_call(
        relay_kernel,
        out_shape=jax.ShapeDtypeStruct((plane,) + got.shape[1:], got.dtype),
        in_specs=[smem, smem, smem, pl.BlockSpec(memory_space=pltpu.VMEM)],
        out_specs=pl.BlockSpec(memory_space=pl.ANY),
        scratch_shapes=[pltpu.SemaphoreType.DMA],
        name="relay_pages",
    )(me, via, dest, got)


def lift_kernel(me_ref, via_ref, own_ref, lifted_ref, sem):
    plane = own_ref.shape[0]
    room = lifted_ref.shape[0]
    group = me_ref[0]
    base = (group // plane) * plane
    place = group % plane

    def visit(act):
        rank = jnp.int32(0)
        for i in range(plane):
            lifted = goes_via(via_ref, base + i, place) & (rank < room)

            @pl.when(lifted)
            def _():
                act(pltpu.make_async_copy(own_ref.at[i], lifted_ref.at[rank], sem))

            rank = rank + jnp.where(lifted, 1, 0)

    visit(lambda copy: copy.start())
    visit(lambda copy: copy.wait())


def lift(me, via, own):
    smem = pl.BlockSpec(memory_space=pltpu.SMEM)
    return pl.pallas_call(
        lift_kernel,
        out_shape=jax.ShapeDtypeStruct((LIFTED,) + own.shape[1:], own.dtype),
        in_specs=[smem, smem, pl.BlockSpec(memory_space=pltpu.VMEM)],
        out_specs=pl.BlockSpec(memory_space=pl.ANY),
        scratch_shapes=[pltpu.SemaphoreType.DMA],
        name="lift_pages",
    )(me, via, own)


def place_early_kernel(me_ref, via_ref, source_ref, own_ref, early_ref, out_ref, sem):
    plane = own_ref.shape[0]
    count, pages = out_ref.shape[:2]
    group = me_ref[0]
    my_half = group // plane

    def visit(act):
        for j in range(count):
            source = source_ref[j]
            near = (source // plane) == my_half
            far = jnp.logical_not(near | goes_via(via_ref, source, group % plane))
            place = source % plane

            @pl.when(near)
            def _():
                act(pltpu.make_async_copy(own_ref.at[place], out_ref.at[j], sem))

            @pl.when(far)
            def _():
                act(
                    pltpu.make_async_copy(
                        early_ref.at[place], out_ref.at[j, pl.ds(0, pages - 1)], sem
                    )
                )

    visit(lambda copy: copy.start())
    visit(lambda copy: copy.wait())


def place_late_kernel(
    me_ref, via_ref, source_ref, late_ref, lifted_ref, _, out_ref, rank_ref, sem
):
    plane = late_ref.shape[0]
    room = lifted_ref.shape[0]
    count, pages = out_ref.shape[:2]
    group = me_ref[0]
    my_half = group // plane
    other = (1 - my_half) * plane
    rank = jnp.int32(0)
    for i in range(plane):
        rank_ref[i] = jnp.minimum(rank, room - 1)
        rank = rank + jnp.where(goes_via(via_ref, other + i, group % plane), 1, 0)

    def visit(act):
        for j in range(count):
            source = source_ref[j]
            place = source % plane
            cross = (source // plane) != my_half
            lifted = cross & goes_via(via_ref, source, group % plane)
            far = cross & jnp.logical_not(lifted)

            @pl.when(far)
            def _():
                act(pltpu.make_async_copy(late_ref.at[place], out_ref.at[j, pages - 1], sem))

            @pl.when(lifted)
            def _():
                act(pltpu.make_async_copy(lifted_ref.at[rank_ref[place]], out_ref.at[j], sem))

    visit(lambda copy: copy.start())
    visit(lambda copy: copy.wait())


def place_early(me, via, sources, own, early):
    smem = pl.BlockSpec(memory_space=pltpu.SMEM)
    vmem = pl.BlockSpec(memory_space=pltpu.VMEM)
    return pl.pallas_call(
        place_early_kernel,
        out_shape=jax.ShapeDtypeStruct((sources.shape[0],) + own.shape[1:], own.dtype),
        in_specs=[smem, smem, smem, vmem, vmem],
        out_specs=pl.BlockSpec(memory_space=pl.ANY),
        scratch_shapes=[pltpu.SemaphoreType.DMA],
        name="place_early",
    )(me, via, sources, own, early)


def place_late(me, via, sources, late, lifted, out):
    smem = pl.BlockSpec(memory_space=pltpu.SMEM)
    vmem = pl.BlockSpec(memory_space=pltpu.VMEM)
    anywhere = pl.BlockSpec(memory_space=pl.ANY)
    return pl.pallas_call(
        place_late_kernel,
        out_shape=jax.ShapeDtypeStruct(out.shape, out.dtype),
        in_specs=[smem, smem, smem, vmem, vmem, anywhere],
        out_specs=anywhere,
        scratch_shapes=[pltpu.SMEM((late.shape[0],), jnp.int32), pltpu.SemaphoreType.DMA],
        input_output_aliases={5: 0},
        name="place_late",
    )(me, via, sources, late, lifted, out)


def local(
    queries,
    fresh_pairs,
    cache_pool,
    out_weight,
    lengths,
    page_table,
    victims,
    victim_dest,
    section_plan,
):
    steps_total = queries.shape[0]
    pool_pages, _, page_len, pair_width = cache_pool.shape[1:]
    kv_heads = pair_width // HEAD_SIZE
    query_heads = queries.shape[3] // HEAD_SIZE
    victim_count = victims.shape[1]
    groups = lax.axis_size("grp")
    ranks = lax.axis_size("tp")
    plane = groups // HALVES
    own_group = lax.axis_index("grp")
    core = lax.axis_index("tp") % 2
    chip = lax.axis_index("tp") // 2
    fresh_steps = fresh_pairs[:, 0]
    pages = cache_pool.reshape(pool_pages, 2 * page_len, pair_width)
    dest = victim_dest.T
    table = page_table[0].T
    plan = section_plan.transpose(2, 1, 0).reshape(steps_total * victim_count, groups)
    sources = jnp.sum(
        jnp.where(dest == own_group, jnp.arange(groups)[None, :], 0), axis=1
    ).astype(jnp.int32)
    me = own_group.astype(jnp.int32)[None]
    half_groups = [list(range(h * plane, (h + 1) * plane)) for h in range(HALVES)]
    swap_halves = [(g, (g + plane) % groups) for g in range(groups)]
    swap_cores = [(r, r ^ 1) for r in range(ranks)]
    chips = ranks // 2
    crossing = (dest // plane) != (jnp.arange(groups) // plane)[None, :]
    bits = jnp.left_shift(jnp.int32(1), dest % plane)
    masks = (
        jnp.sum(jnp.where(crossing, 0, bits), axis=0),
        jnp.sum(jnp.where(crossing, bits, 0), axis=0),
        jnp.sum(crossing.astype(jnp.int32), axis=0),
    )

    def in_half(slots):
        return lax.all_to_all(slots, "grp", 0, 0, axis_index_groups=half_groups, tiled=True)

    def swap(slots):
        return lax.ppermute(slots, "grp", swap_halves)

    def pack_args(via):
        return (me, via, lengths, table, victims, dest, plan)

    early, via = first_pages(STRAIGHT, me, masks, table, victims, dest, pages, steps_total - 1)
    early_got = swap(early)
    own, late = pack(STRAIGHT, pack_args(via), fresh_steps, pages, plane, early)
    own_got = in_half(own)
    attended = attend_all(
        queries[:, 0],
        fresh_steps,
        cache_pool[0],
        page_table[0],
        lengths[0],
        kv_heads,
        query_heads,
    )
    stacked = jnp.moveaxis(attended, 0, 1)
    partial = jnp.einsum("rsk,kd->rsd", stacked, out_weight, preferred_element_type=jnp.float32)
    by_core = partial.reshape((chips, 2, -1) + partial.shape[1:])
    kept = lax.dynamic_index_in_dim(by_core, core, 1, keepdims=False)
    given = lax.dynamic_index_in_dim(by_core, 1 - core, 1, keepdims=False)
    on_chip = kept + lax.ppermute(given, "tp", swap_cores)
    projected = lax.dynamic_index_in_dim(on_chip, chip, 0, keepdims=False)
    on_chip = on_chip.astype(jnp.bfloat16)
    for shift in range(1, chips):
        share = lax.dynamic_index_in_dim(on_chip, (chip + shift) % chips, 0, keepdims=False)
        share = lax.ppermute(
            share, "tp", [(r, (r + 2 * shift) % ranks) for r in range(ranks)]
        )
        projected = projected + share.astype(jnp.float32)
    projected = projected.astype(jnp.bfloat16)

    late, on_chip = lax.optimization_barrier((late, on_chip))
    late_got = swap(late)
    early_slots = relay(me, via, dest, early_got, plane)
    early_slots, own_got = lax.optimization_barrier((early_slots, own_got))
    early_arrived = in_half(early_slots)
    lifted = lift(me, via, own_got)
    lifted, early_arrived = lax.optimization_barrier((lifted, early_arrived))
    lifted_got = swap(lifted)
    migrated = place_early(me, via, sources, own_got, early_arrived)
    late_slots = relay(me, via, dest, late_got, plane)
    late_slots, early_arrived = lax.optimization_barrier((late_slots, early_arrived))
    late_arrived = in_half(late_slots)
    migrated = place_late(me, via, sources, late_arrived, lifted_got, migrated)

    def straight_only(carry):
        no_via = jnp.zeros_like(via)
        early, _ = first_pages(
            victim_count, me, masks, table, victims, dest, pages, steps_total - 1
        )
        own, late = pack(victim_count, pack_args(no_via), fresh_steps, pages, plane, early)
        own_got = in_half(own)
        early_arrived = in_half(relay(me, no_via, dest, swap(early), plane))
        late_arrived = in_half(relay(me, no_via, dest, swap(late), plane))
        out = place_early(me, no_via, sources, own_got, early_arrived)
        lifted = jnp.zeros((LIFTED,) + own.shape[1:], own.dtype)
        return jnp.int32(0), place_late(me, no_via, sources, late_arrived, lifted, out)

    _, migrated = lax.while_loop(lambda c: c[0] > 0, straight_only, (via[groups], migrated))
    migrated = migrated.reshape(1, victim_count, steps_total, 2, page_len, pair_width)
    return (projected[None], migrated)


def solution(mesh):
    return jax.shard_map(
        local,
        mesh=mesh,
        in_specs=(
            P(None, "grp", None, "tp"),
            P(None, "grp", None, None, "tp"),
            P("grp", None, None, None, "tp"),
            P("tp", None),
            P("grp", None),
            P("grp", None, None),
            P("grp", None),
            P(),
            P(),
        ),
        out_specs=(P("grp", "tp", None, None), P("grp", None, None, None, None, "tp")),
        check_vma=False,
    )
```

```python
import functools
import math

import jax
import jax.numpy as jnp
from jax import lax
from jax.experimental import pallas as pl
from jax.experimental.pallas import tpu as pltpu
from jax.sharding import PartitionSpec as P

HEAD_SIZE = 128
HALVES = 2
STRAIGHT = 8
LIFTED = 2
RELAY_FIRST = 20.3
RELAY_LAST = 20
PLACE_FIRST = 15
ALL_VMEM = 62 * 2**20
FREE = pl.CostEstimate(flops=0, bytes_accessed=0, transcendentals=0)


masked_score = -1e30


def attend_kernel(
    per_rank,
    core_ref,
    length_ref,
    table_ref,
    query_ref,
    fresh_ref,
    cache_ref,
    weight_ref,
    _,
    kept_ref,
    given_ref,
    pool,
    weight,
    attended,
    sems,
):
    entries, requests = table_ref.shape
    steps = fresh_ref.shape[2]
    page_len = cache_ref.shape[1] // 2
    padded = query_ref.shape[1]
    heads = attended.shape[2] // HEAD_SIZE
    pool_in = pltpu.make_async_copy(cache_ref, pool, sems.at[0])
    weight_in = pltpu.make_async_copy(weight_ref, weight, sems.at[1])
    pool_in.start()
    weight_in.start()
    attended[...] = jnp.zeros_like(attended)
    pool_in.wait()
    tile = 16
    tile_rows = lax.broadcasted_iota(jnp.int32, (tile, HEAD_SIZE), 0)
    columns = lax.broadcasted_iota(jnp.int32, (padded, entries * page_len), 1)
    row_steps = lax.broadcasted_iota(jnp.int32, (padded, entries * page_len), 0) // heads
    scale = 1.0 / math.sqrt(HEAD_SIZE)
    for r in range(requests):
        length = length_ref[0, r]
        for t in range(steps):
            position = length + t
            page = table_ref[position // page_len, r]
            row = position % page_len
            base = (row // tile) * tile
            for side in range(2):
                span = pl.ds(pl.multiple_of(side * page_len + base, tile), tile)
                token = fresh_ref[r, side].astype(jnp.float32)[t : t + 1]
                content = pool[page, span, :].astype(jnp.float32)
                content = jnp.where(tile_rows == row - base, token, content)
                pool[page, span, :] = content.astype(jnp.bfloat16)
    for r in range(requests):
        length = length_ref[0, r]
        query = query_ref[r]
        scores = jnp.concatenate(
            [
                lax.dot_general(
                    query,
                    pool[table_ref[p, r], pl.ds(0, page_len), :],
                    (((1,), (1,)), ((), ())),
                    preferred_element_type=jnp.float32,
                )
                for p in range(entries)
            ],
            axis=1,
        )
        scores = jnp.where(columns <= length + row_steps, scores * scale, masked_score)
        weights = jnp.exp(scores - jnp.max(scores, axis=1, keepdims=True))
        total = jnp.sum(weights, axis=1, keepdims=True)
        probs = weights.astype(jnp.bfloat16)
        summed = jnp.zeros((padded, HEAD_SIZE), jnp.float32)
        for p in range(entries):
            summed = summed + jnp.dot(
                probs[:, p * page_len : (p + 1) * page_len],
                pool[table_ref[p, r], pl.ds(page_len, page_len), :],
                preferred_element_type=jnp.float32,
            )
        result = (summed / total).astype(jnp.bfloat16).astype(jnp.float32)
        block, place = divmod(r, per_rank)
        side = (block % 2) ^ core_ref[0]
        for t in range(steps):
            row = ((block // 2) * per_rank + place) * steps + t
            for h in range(heads):
                attended[side, row, pl.ds(h * HEAD_SIZE, HEAD_SIZE)] = result[t * heads + h]
    weight_in.wait()
    rows = kept_ref.shape[0]
    left = attended[...].astype(jnp.bfloat16)
    width = 512

    def project(n, carry):
        span = pl.ds(pl.multiple_of(n * width, width), width)
        for side, out_ref in enumerate((kept_ref, given_ref)):
            product = jnp.dot(left[side], weight[:, span], preferred_element_type=jnp.float32)
            out_ref[:, span] = product[:rows]
        return carry

    lax.fori_loop(0, weight.shape[1] // width, project, 0)


def attend(core, lengths, table, queries, fresh, cache, out_weight, ranks, after):
    steps, requests, features = queries.shape
    heads = features // HEAD_SIZE
    by_request = queries.reshape(steps, requests, heads, HEAD_SIZE).transpose(1, 0, 2, 3)
    by_request = by_request.reshape(requests, steps * heads, HEAD_SIZE)
    by_request = jnp.pad(by_request, ((0, 0), (0, -(steps * heads) % 16), (0, 0)))
    fresh = fresh.transpose(1, 2, 0, 3)
    rows = requests * steps // 2
    padded = rows + (-rows) % 8
    smem = pl.BlockSpec(memory_space=pltpu.SMEM)
    vmem = pl.BlockSpec(memory_space=pltpu.VMEM)
    anywhere = pl.BlockSpec(memory_space=pl.ANY)
    half = jax.ShapeDtypeStruct((rows, out_weight.shape[1]), jnp.float32)
    return pl.pallas_call(
        functools.partial(attend_kernel, requests // ranks),
        out_shape=(half, half),
        in_specs=[smem, smem, smem, vmem, vmem, anywhere, anywhere, anywhere],
        out_specs=(vmem, vmem),
        scratch_shapes=[
            pltpu.VMEM(cache.shape, cache.dtype),
            pltpu.VMEM(out_weight.shape, out_weight.dtype),
            pltpu.VMEM((2, padded, features), jnp.float32),
            pltpu.SemaphoreType.DMA((2,)),
        ],
        compiler_params=pltpu.CompilerParams(vmem_limit_bytes=40 * 2**20),
        cost_estimate=FREE,
        name="attend_and_project",
    )(core, lengths, table, by_request, fresh, cache, out_weight, after)


def route(own_ref, cross_ref, count_ref, via_ref, half, plane, straight):
    def source(i, carry):
        s = half * plane + i

        def pick(_, state):
            free, chosen, once, twice, bad = state
            empty = free & ~once
            pool = jnp.where(empty != 0, empty, free & ~twice)
            bit = pool & -pool
            twice = twice | (once & bit)
            return free & ~bit, chosen | bit, once | bit, twice, bad | (bit == 0).astype(jnp.int32)

        once, twice, bad = carry
        free = cross_ref[s] & ~own_ref[s]
        extra = jnp.maximum(count_ref[s] - straight, 0)
        _, chosen, once, twice, bad = lax.fori_loop(
            0, extra, pick, (free, jnp.int32(0), once, twice, bad)
        )
        via_ref[s] = chosen
        return once, twice, bad

    zero = jnp.int32(0)
    return lax.fori_loop(0, plane, source, (zero, zero, zero))[2]


def goes_via(via_ref, source, place):
    return ((via_ref[source] >> place) & 1) == 1


def first_pages_kernel(
    me_ref,
    own_ref,
    cross_ref,
    count_ref,
    table_ref,
    victim_ref,
    dest_ref,
    cache_ref,
    early_ref,
    via_ref,
    held,
    in_sem,
    out_sem,
):
    count, pages = held.shape[:2]
    groups = dest_ref.shape[1]
    plane = groups // HALVES
    straight = early_ref.shape[0]
    group = me_ref[0]
    my_half = group // plane

    def page_in(j, p):
        page = table_ref[p, victim_ref[0, j]]
        return pltpu.make_async_copy(cache_ref.at[page], held.at[j, p], in_sem.at[j])

    def copy_out(j, rank):
        return pltpu.make_async_copy(held.at[j], early_ref.at[rank], out_sem)

    def visit(act):
        rank = jnp.int32(0)
        for j in range(count):
            target = dest_ref[j, group]
            leaves = ((target // plane) != my_half) & jnp.logical_not(
                goes_via(via_ref, group, target % plane)
            )
            leaves = leaves & (rank < straight)

            @pl.when(leaves)
            def _():
                act(j, rank)

            rank = rank + jnp.where(leaves, 1, 0)

    def read(j, rank):
        for p in range(pages):
            page_in(j, p).start()

    def write(j, rank):
        for p in range(pages):
            page_in(j, p).wait()
        copy_out(j, rank).start()

    bad = route(own_ref, cross_ref, count_ref, via_ref, my_half, plane, straight)
    visit(read)
    bad = bad | route(own_ref, cross_ref, count_ref, via_ref, 1 - my_half, plane, straight)
    via_ref[groups] = bad
    visit(write)
    visit(lambda j, rank: copy_out(j, rank).wait())


def first_pages(straight, me, masks, table, victims, dest, cache, pages):
    count = victims.shape[1]
    groups = dest.shape[1]
    smem = pl.BlockSpec(memory_space=pltpu.SMEM)
    anywhere = pl.BlockSpec(memory_space=pl.ANY)
    return pl.pallas_call(
        first_pages_kernel,
        out_shape=(
            jax.ShapeDtypeStruct((straight, pages) + cache.shape[1:], cache.dtype),
            jax.ShapeDtypeStruct((groups + 1,), jnp.int32),
        ),
        in_specs=[smem] * 7 + [anywhere],
        out_specs=(anywhere, smem),
        scratch_shapes=[
            pltpu.VMEM((count, pages) + cache.shape[1:], cache.dtype),
            pltpu.SemaphoreType.DMA((count,)),
            pltpu.SemaphoreType.DMA,
        ],
        cost_estimate=FREE,
        name="first_pages",
    )(me, *masks, table, victims, dest, cache)


def pack_kernel(
    me_ref,
    via_ref,
    length_ref,
    table_ref,
    victim_ref,
    dest_ref,
    plan_ref,
    fresh_ref,
    cache_ref,
    _,
    own_ref,
    late_ref,
    held,
    in_sem,
    out_sem,
):
    count, pages, rows, _ = held.shape
    steps = fresh_ref.shape[0]
    page_len = rows // 2
    plane = own_ref.shape[0]
    straight = late_ref.shape[0]
    group = me_ref[0]
    my_half = group // plane

    def page_in(j, p):
        page = table_ref[p, victim_ref[0, j]]
        return pltpu.make_async_copy(cache_ref.at[page], held.at[j, p], in_sem.at[j])

    def send(j, rank, act):
        target = dest_ref[j, group]
        place = target % plane
        in_half = ((target // plane) == my_half) | goes_via(via_ref, group, place)
        leaves = jnp.logical_not(in_half) & (rank < straight)

        @pl.when(in_half)
        def _():
            act(pltpu.make_async_copy(held.at[j], own_ref.at[place], out_sem))

        @pl.when(leaves)
        def _():
            act(pltpu.make_async_copy(held.at[j, pages - 1], late_ref.at[rank], out_sem))

        return rank + jnp.where(leaves, 1, 0)

    for j in range(count):
        for p in range(pages):
            page_in(j, p).start()
    row_ids = lax.broadcasted_iota(jnp.int32, (page_len, HEAD_SIZE), 0)
    rank = jnp.int32(0)
    for j in range(count):
        for p in range(pages):
            page_in(j, p).wait()
        victim = victim_ref[0, j]
        first = length_ref[0, victim] - (pages - 1) * page_len
        last_step = jnp.int32(0)
        for s in range(steps):
            last_step = jnp.where(plan_ref[s * count + j, group] == pages - 1, s, last_step)
        for side in range(2):
            span = pl.ds(side * page_len, page_len)
            content = held[j, pages - 1, span, :].astype(jnp.float32)
            for t in range(steps):
                row = jnp.where(t <= last_step, first + t, -1)
                token = fresh_ref[t, victim].astype(jnp.float32)[side : side + 1]
                content = jnp.where(row_ids == row, token, content)
            held[j, pages - 1, span, :] = content.astype(jnp.bfloat16)
        rank = send(j, rank, lambda copy: copy.start())
    rank = jnp.int32(0)
    for j in range(count):
        rank = send(j, rank, lambda copy: copy.wait())


def pack(straight, scalars, fresh, cache, plane, early):
    count = scalars[4].shape[1]
    steps = fresh.shape[0]
    rows, width = cache.shape[1:]
    smem = pl.BlockSpec(memory_space=pltpu.SMEM)
    anywhere = pl.BlockSpec(memory_space=pl.ANY)
    return pl.pallas_call(
        pack_kernel,
        out_shape=(
            jax.ShapeDtypeStruct((plane, steps, rows, width), cache.dtype),
            jax.ShapeDtypeStruct((straight, rows, width), cache.dtype),
        ),
        in_specs=[smem] * 7 + [pl.BlockSpec(memory_space=pltpu.VMEM), anywhere, anywhere],
        out_specs=(anywhere,) * 2,
        scratch_shapes=[
            pltpu.VMEM((count, steps, rows, width), cache.dtype),
            pltpu.SemaphoreType.DMA((count,)),
            pltpu.SemaphoreType.DMA,
        ],
        cost_estimate=FREE,
        name="pack_pages",
    )(*scalars, fresh, cache, early)


def relay_kernel(me_ref, via_ref, dest_ref, got_ref, slots_ref, sem):
    plane = slots_ref.shape[0]
    count = dest_ref.shape[0]
    straight = got_ref.shape[0]
    group = me_ref[0]
    my_half = group // plane
    partner = jnp.where(group < plane, group + plane, group - plane)

    def visit(act):
        rank = jnp.int32(0)
        for j in range(count):
            target = dest_ref[j, partner]
            place = target % plane
            came = ((target // plane) == my_half) & jnp.logical_not(
                goes_via(via_ref, partner, place)
            )
            came = came & (rank < straight)

            @pl.when(came)
            def _():
                act(pltpu.make_async_copy(got_ref.at[rank], slots_ref.at[place], sem))

            rank = rank + jnp.where(came, 1, 0)

    visit(lambda copy: copy.start())
    visit(lambda copy: copy.wait())


def cost(microseconds):
    return pl.CostEstimate(flops=int(microseconds * 10**9), bytes_accessed=0, transcendentals=0)


def relay(me, via, dest, got, plane, guess):
    smem = pl.BlockSpec(memory_space=pltpu.SMEM)
    return pl.pallas_call(
        relay_kernel,
        out_shape=jax.ShapeDtypeStruct((plane,) + got.shape[1:], got.dtype),
        in_specs=[smem, smem, smem, pl.BlockSpec(memory_space=pltpu.VMEM)],
        out_specs=pl.BlockSpec(memory_space=pl.ANY),
        scratch_shapes=[pltpu.SemaphoreType.DMA],
        cost_estimate=cost(guess),
        name="relay_pages",
    )(me, via, dest, got)


def lift_kernel(me_ref, via_ref, own_ref, lifted_ref, sem):
    plane = own_ref.shape[0]
    room = lifted_ref.shape[0]
    group = me_ref[0]
    base = (group // plane) * plane
    place = group % plane

    def visit(act):
        rank = jnp.int32(0)
        for i in range(plane):
            lifted = goes_via(via_ref, base + i, place) & (rank < room)

            @pl.when(lifted)
            def _():
                act(pltpu.make_async_copy(own_ref.at[i], lifted_ref.at[rank], sem))

            rank = rank + jnp.where(lifted, 1, 0)

    visit(lambda copy: copy.start())
    visit(lambda copy: copy.wait())


def lift(me, via, own):
    smem = pl.BlockSpec(memory_space=pltpu.SMEM)
    return pl.pallas_call(
        lift_kernel,
        out_shape=jax.ShapeDtypeStruct((LIFTED,) + own.shape[1:], own.dtype),
        in_specs=[smem, smem, pl.BlockSpec(memory_space=pltpu.VMEM)],
        out_specs=pl.BlockSpec(memory_space=pl.ANY),
        scratch_shapes=[pltpu.SemaphoreType.DMA],
        cost_estimate=FREE,
        name="lift_pages",
    )(me, via, own)


def place_first_kernel(
    me_ref, via_ref, source_ref, own_ref, early_ref, lifted_ref, out_ref, rank_ref, sem
):
    plane = own_ref.shape[0]
    room = lifted_ref.shape[0]
    count, pages = out_ref.shape[:2]
    group = me_ref[0]
    my_half = group // plane
    other = (1 - my_half) * plane
    rank = jnp.int32(0)
    for i in range(plane):
        rank_ref[i] = jnp.minimum(rank, room - 1)
        rank = rank + jnp.where(goes_via(via_ref, other + i, group % plane), 1, 0)

    def visit(act):
        for j in range(count):
            source = source_ref[j]
            place = source % plane
            near = (source // plane) == my_half
            via = goes_via(via_ref, source, group % plane)
            lifted = jnp.logical_not(near) & via
            far = jnp.logical_not(near | via)

            @pl.when(near)
            def _():
                act(pltpu.make_async_copy(own_ref.at[place], out_ref.at[j], sem))

            @pl.when(far)
            def _():
                act(
                    pltpu.make_async_copy(
                        early_ref.at[place], out_ref.at[j, pl.ds(0, pages - 1)], sem
                    )
                )

            @pl.when(lifted)
            def _():
                act(pltpu.make_async_copy(lifted_ref.at[rank_ref[place]], out_ref.at[j], sem))

    visit(lambda copy: copy.start())
    visit(lambda copy: copy.wait())


def place_late_kernel(me_ref, via_ref, source_ref, late_ref, _, out_ref, sem):
    plane = late_ref.shape[0]
    count, pages = out_ref.shape[:2]
    group = me_ref[0]
    my_half = group // plane

    def visit(act):
        for j in range(count):
            source = source_ref[j]
            place = source % plane
            near = (source // plane) == my_half
            far = jnp.logical_not(near | goes_via(via_ref, source, group % plane))

            @pl.when(far)
            def _():
                act(pltpu.make_async_copy(late_ref.at[place], out_ref.at[j, pages - 1], sem))

    visit(lambda copy: copy.start())
    visit(lambda copy: copy.wait())


def place_first(me, via, sources, own, early, lifted):
    smem = pl.BlockSpec(memory_space=pltpu.SMEM)
    vmem = pl.BlockSpec(memory_space=pltpu.VMEM)
    return pl.pallas_call(
        place_first_kernel,
        out_shape=jax.ShapeDtypeStruct((sources.shape[0],) + own.shape[1:], own.dtype),
        in_specs=[smem, smem, smem, vmem, vmem, vmem],
        out_specs=pl.BlockSpec(memory_space=pltpu.HBM),
        scratch_shapes=[pltpu.SMEM((own.shape[0],), jnp.int32), pltpu.SemaphoreType.DMA],
        compiler_params=pltpu.CompilerParams(vmem_limit_bytes=ALL_VMEM),
        cost_estimate=cost(PLACE_FIRST),
        name="place_first",
    )(me, via, sources, own, early, lifted)


def place_late(me, via, sources, late, out):
    smem = pl.BlockSpec(memory_space=pltpu.SMEM)
    hbm = pl.BlockSpec(memory_space=pltpu.HBM)
    return pl.pallas_call(
        place_late_kernel,
        out_shape=jax.ShapeDtypeStruct(out.shape, out.dtype),
        in_specs=[smem, smem, smem, pl.BlockSpec(memory_space=pltpu.VMEM), hbm],
        out_specs=hbm,
        scratch_shapes=[pltpu.SemaphoreType.DMA],
        input_output_aliases={4: 0},
        compiler_params=pltpu.CompilerParams(vmem_limit_bytes=ALL_VMEM),
        cost_estimate=FREE,
        name="place_late",
    )(me, via, sources, late, out)


def local(
    queries,
    fresh_pairs,
    cache_pool,
    out_weight,
    lengths,
    page_table,
    victims,
    victim_dest,
    section_plan,
):
    steps_total = queries.shape[0]
    pool_pages, _, page_len, pair_width = cache_pool.shape[1:]
    victim_count = victims.shape[1]
    groups = lax.axis_size("grp")
    ranks = lax.axis_size("tp")
    plane = groups // HALVES
    own_group = lax.axis_index("grp")
    core = lax.axis_index("tp") % 2
    chip = lax.axis_index("tp") // 2
    fresh_steps = fresh_pairs[:, 0]
    pages = cache_pool.reshape(pool_pages, 2 * page_len, pair_width)
    dest = victim_dest.T
    table = page_table[0].T
    plan = section_plan.transpose(2, 1, 0).reshape(steps_total * victim_count, groups)
    sources = jnp.sum(
        jnp.where(dest == own_group, jnp.arange(groups)[None, :], 0), axis=1
    ).astype(jnp.int32)
    me = own_group.astype(jnp.int32)[None]
    half_groups = [list(range(h * plane, (h + 1) * plane)) for h in range(HALVES)]
    swap_halves = [(g, (g + plane) % groups) for g in range(groups)]
    swap_cores = [(r, r ^ 1) for r in range(ranks)]
    chips = ranks // 2
    crossing = (dest // plane) != (jnp.arange(groups) // plane)[None, :]
    bits = jnp.left_shift(jnp.int32(1), dest % plane)
    masks = (
        jnp.sum(jnp.where(crossing, 0, bits), axis=0),
        jnp.sum(jnp.where(crossing, bits, 0), axis=0),
        jnp.sum(crossing.astype(jnp.int32), axis=0),
    )

    def in_half(slots):
        return lax.all_to_all(slots, "grp", 0, 0, axis_index_groups=half_groups, tiled=True)

    def swap(slots):
        return lax.ppermute(slots, "grp", swap_halves)

    def pack_args(via):
        return (me, via, lengths, table, victims, dest, plan)

    early, via = first_pages(STRAIGHT, me, masks, table, victims, dest, pages, steps_total - 1)
    early_got = swap(early)
    own, late = pack(STRAIGHT, pack_args(via), fresh_steps, pages, plane, early)
    own_got = in_half(own)
    kept, given = attend(
        core.astype(jnp.int32)[None],
        lengths,
        table,
        queries[:, 0],
        fresh_steps,
        pages,
        out_weight,
        ranks,
        own,
    )
    on_chip = kept + lax.ppermute(given, "tp", swap_cores)
    on_chip = on_chip.reshape(chips, -1, steps_total, on_chip.shape[1])
    late, on_chip = lax.optimization_barrier((late, on_chip))
    late_got = swap(late)
    projected = lax.dynamic_index_in_dim(on_chip, chip, 0, keepdims=False)
    on_chip = on_chip.astype(jnp.bfloat16)
    for shift in range(1, chips):
        share = lax.dynamic_index_in_dim(on_chip, (chip + shift) % chips, 0, keepdims=False)
        share = lax.ppermute(
            share, "tp", [(r, (r + 2 * shift) % ranks) for r in range(ranks)]
        )
        projected = projected + share.astype(jnp.float32)
    projected = projected.astype(jnp.bfloat16)

    early_slots = relay(me, via, dest, early_got, plane, RELAY_FIRST)
    early_arrived = in_half(early_slots)
    lifted = lift(me, via, own_got)
    lifted, late_got, projected = lax.optimization_barrier((lifted, late_got, projected))
    lifted_got = swap(lifted)
    migrated = place_first(me, via, sources, own_got, early_arrived, lifted_got)
    late_slots = relay(me, via, dest, late_got, plane, RELAY_LAST)
    late_arrived = in_half(late_slots)
    migrated = place_late(me, via, sources, late_arrived, migrated)

    def straight_only(carry):
        no_via = jnp.zeros_like(via)
        early, _ = first_pages(
            victim_count, me, masks, table, victims, dest, pages, steps_total - 1
        )
        own, late = pack(victim_count, pack_args(no_via), fresh_steps, pages, plane, early)
        own_got = in_half(own)
        early_arrived = in_half(relay(me, no_via, dest, swap(early), plane, 0))
        late_arrived = in_half(relay(me, no_via, dest, swap(late), plane, 0))
        lifted = jnp.zeros((LIFTED,) + own.shape[1:], own.dtype)
        out = place_first(me, no_via, sources, own_got, early_arrived, lifted)
        return jnp.int32(0), place_late(me, no_via, sources, late_arrived, out)

    _, migrated = lax.while_loop(lambda c: c[0] > 0, straight_only, (via[groups], migrated))
    migrated = migrated.reshape(1, victim_count, steps_total, 2, page_len, pair_width)
    return (projected[None], migrated)


def solution(mesh):
    return jax.shard_map(
        local,
        mesh=mesh,
        in_specs=(
            P(None, "grp", None, "tp"),
            P(None, "grp", None, None, "tp"),
            P("grp", None, None, None, "tp"),
            P("tp", None),
            P("grp", None),
            P("grp", None, None),
            P("grp", None),
            P(),
            P(),
        ),
        out_specs=(P("grp", "tp", None, None), P("grp", None, None, None, None, "tp")),
        check_vma=False,
    )
```

```python
import functools
import math

import jax
import jax.numpy as jnp
from jax import lax
from jax.experimental import pallas as pl
from jax.experimental.pallas import tpu as pltpu
from jax.sharding import PartitionSpec as P

HEAD_SIZE = 128
HALVES = 2
STRAIGHT = 8
LIFTED = 2
RELAY_FIRST = 20.3
RELAY_LAST = 18
PLACE_FIRST = 15
ALL_VMEM = 62 * 2**20
FREE = pl.CostEstimate(flops=0, bytes_accessed=0, transcendentals=0)


masked_score = -1e30


def attend_kernel(
    per_rank,
    core_ref,
    length_ref,
    table_ref,
    query_ref,
    fresh_ref,
    cache_ref,
    weight_ref,
    _,
    kept_ref,
    given_ref,
    pool,
    weight,
    attended,
    sems,
):
    entries, requests = table_ref.shape
    steps = fresh_ref.shape[2]
    page_len = cache_ref.shape[1] // 2
    padded = query_ref.shape[1]
    heads = attended.shape[2] // HEAD_SIZE
    pool_in = pltpu.make_async_copy(cache_ref, pool, sems.at[0])
    weight_in = pltpu.make_async_copy(weight_ref, weight, sems.at[1])
    pool_in.start()
    weight_in.start()
    attended[...] = jnp.zeros_like(attended)
    pool_in.wait()
    tile = 16
    tile_rows = lax.broadcasted_iota(jnp.int32, (tile, HEAD_SIZE), 0)
    columns = lax.broadcasted_iota(jnp.int32, (padded, entries * page_len), 1)
    row_steps = lax.broadcasted_iota(jnp.int32, (padded, entries * page_len), 0) // heads
    scale = 1.0 / math.sqrt(HEAD_SIZE)
    for r in range(requests):
        length = length_ref[0, r]
        for t in range(steps):
            position = length + t
            page = table_ref[position // page_len, r]
            row = position % page_len
            base = (row // tile) * tile
            for side in range(2):
                span = pl.ds(pl.multiple_of(side * page_len + base, tile), tile)
                token = fresh_ref[r, side].astype(jnp.float32)[t : t + 1]
                content = pool[page, span, :].astype(jnp.float32)
                content = jnp.where(tile_rows == row - base, token, content)
                pool[page, span, :] = content.astype(jnp.bfloat16)
    for r in range(requests):
        length = length_ref[0, r]
        query = query_ref[r]
        scores = jnp.concatenate(
            [
                lax.dot_general(
                    query,
                    pool[table_ref[p, r], pl.ds(0, page_len), :],
                    (((1,), (1,)), ((), ())),
                    preferred_element_type=jnp.float32,
                )
                for p in range(entries)
            ],
            axis=1,
        )
        scores = jnp.where(columns <= length + row_steps, scores * scale, masked_score)
        weights = jnp.exp(scores - jnp.max(scores, axis=1, keepdims=True))
        total = jnp.sum(weights, axis=1, keepdims=True)
        probs = weights.astype(jnp.bfloat16)
        summed = jnp.zeros((padded, HEAD_SIZE), jnp.float32)
        for p in range(entries):
            summed = summed + jnp.dot(
                probs[:, p * page_len : (p + 1) * page_len],
                pool[table_ref[p, r], pl.ds(page_len, page_len), :],
                preferred_element_type=jnp.float32,
            )
        result = (summed / total).astype(jnp.bfloat16).astype(jnp.float32)
        block, place = divmod(r, per_rank)
        side = (block % 2) ^ core_ref[0]
        for t in range(steps):
            row = ((block // 2) * per_rank + place) * steps + t
            for h in range(heads):
                attended[side, row, pl.ds(h * HEAD_SIZE, HEAD_SIZE)] = result[t * heads + h]
    weight_in.wait()
    rows = kept_ref.shape[0]
    left = attended[...].astype(jnp.bfloat16)
    width = 512

    def project(n, carry):
        span = pl.ds(pl.multiple_of(n * width, width), width)
        for side, out_ref in enumerate((kept_ref, given_ref)):
            product = jnp.dot(left[side], weight[:, span], preferred_element_type=jnp.float32)
            out_ref[:, span] = product[:rows]
        return carry

    lax.fori_loop(0, weight.shape[1] // width, project, 0)


def attend(core, lengths, table, queries, fresh, cache, out_weight, ranks, after):
    steps, requests, features = queries.shape
    heads = features // HEAD_SIZE
    by_request = queries.reshape(steps, requests, heads, HEAD_SIZE).transpose(1, 0, 2, 3)
    by_request = by_request.reshape(requests, steps * heads, HEAD_SIZE)
    by_request = jnp.pad(by_request, ((0, 0), (0, -(steps * heads) % 16), (0, 0)))
    fresh = fresh.transpose(1, 2, 0, 3)
    rows = requests * steps // 2
    padded = rows + (-rows) % 8
    smem = pl.BlockSpec(memory_space=pltpu.SMEM)
    vmem = pl.BlockSpec(memory_space=pltpu.VMEM)
    anywhere = pl.BlockSpec(memory_space=pl.ANY)
    half = jax.ShapeDtypeStruct((rows, out_weight.shape[1]), jnp.float32)
    return pl.pallas_call(
        functools.partial(attend_kernel, requests // ranks),
        out_shape=(half, half),
        in_specs=[smem, smem, smem, vmem, vmem, anywhere, anywhere, anywhere],
        out_specs=(vmem, vmem),
        scratch_shapes=[
            pltpu.VMEM(cache.shape, cache.dtype),
            pltpu.VMEM(out_weight.shape, out_weight.dtype),
            pltpu.VMEM((2, padded, features), jnp.float32),
            pltpu.SemaphoreType.DMA((2,)),
        ],
        compiler_params=pltpu.CompilerParams(vmem_limit_bytes=40 * 2**20),
        cost_estimate=FREE,
        name="attend_and_project",
    )(core, lengths, table, by_request, fresh, cache, out_weight, after)


def route(own_ref, cross_ref, count_ref, via_ref, half, plane, straight):
    def source(i, carry):
        s = half * plane + i

        def pick(_, state):
            free, chosen, once, twice, bad = state
            empty = free & ~once
            pool = jnp.where(empty != 0, empty, free & ~twice)
            bit = pool & -pool
            twice = twice | (once & bit)
            return free & ~bit, chosen | bit, once | bit, twice, bad | (bit == 0).astype(jnp.int32)

        once, twice, bad = carry
        free = cross_ref[s] & ~own_ref[s]
        extra = jnp.maximum(count_ref[s] - straight, 0)
        _, chosen, once, twice, bad = lax.fori_loop(
            0, extra, pick, (free, jnp.int32(0), once, twice, bad)
        )
        via_ref[s] = chosen
        return once, twice, bad

    zero = jnp.int32(0)
    return lax.fori_loop(0, plane, source, (zero, zero, zero))[2]


def goes_via(via_ref, source, place):
    return ((via_ref[source] >> place) & 1) == 1


def pack_kernel(
    me_ref,
    own_mask_ref,
    cross_mask_ref,
    count_ref,
    length_ref,
    table_ref,
    victim_ref,
    dest_ref,
    plan_ref,
    fresh_ref,
    cache_ref,
    via_ref,
    early_ref,
    late_ref,
    own_ref,
    held,
    in_sem,
    out_sem,
):
    count, pages, rows, _ = held.shape
    steps = fresh_ref.shape[0]
    page_len = rows // 2
    groups = dest_ref.shape[1]
    plane = own_ref.shape[0]
    straight = late_ref.shape[0]
    group = me_ref[0]
    my_half = group // plane

    def page_in(j, p):
        page = table_ref[p, victim_ref[0, j]]
        return pltpu.make_async_copy(cache_ref.at[page], held.at[j, p], in_sem.at[j])

    def send(j, rank, act):
        target = dest_ref[j, group]
        place = target % plane
        in_half = ((target // plane) == my_half) | goes_via(via_ref, group, place)
        leaves = jnp.logical_not(in_half) & (rank < straight)

        @pl.when(in_half)
        def _():
            act(pltpu.make_async_copy(held.at[j], own_ref.at[place], out_sem))

        @pl.when(leaves)
        def _():
            act(
                pltpu.make_async_copy(
                    held.at[j, pl.ds(0, pages - 1)], early_ref.at[rank], out_sem
                )
            )
            act(pltpu.make_async_copy(held.at[j, pages - 1], late_ref.at[rank], out_sem))

        return rank + jnp.where(leaves, 1, 0)

    for j in range(count):
        for p in range(pages):
            page_in(j, p).start()
    masks = (own_mask_ref, cross_mask_ref, count_ref, via_ref)
    bad = route(*masks, my_half, plane, straight)
    via_ref[groups] = bad | route(*masks, 1 - my_half, plane, straight)
    row_ids = lax.broadcasted_iota(jnp.int32, (page_len, HEAD_SIZE), 0)
    rank = jnp.int32(0)
    for j in range(count):
        for p in range(pages):
            page_in(j, p).wait()
        victim = victim_ref[0, j]
        first = length_ref[0, victim] - (pages - 1) * page_len
        last_step = jnp.int32(0)
        for s in range(steps):
            last_step = jnp.where(plan_ref[s * count + j, group] == pages - 1, s, last_step)
        for side in range(2):
            span = pl.ds(side * page_len, page_len)
            content = held[j, pages - 1, span, :].astype(jnp.float32)
            for t in range(steps):
                row = jnp.where(t <= last_step, first + t, -1)
                token = fresh_ref[t, victim].astype(jnp.float32)[side : side + 1]
                content = jnp.where(row_ids == row, token, content)
            held[j, pages - 1, span, :] = content.astype(jnp.bfloat16)
        rank = send(j, rank, lambda copy: copy.start())
    rank = jnp.int32(0)
    for j in range(count):
        rank = send(j, rank, lambda copy: copy.wait())


def pack(straight, scalars, fresh, cache, plane):
    dest = scalars[7]
    count, groups = dest.shape
    steps = fresh.shape[0]
    rows, width = cache.shape[1:]
    smem = pl.BlockSpec(memory_space=pltpu.SMEM)
    anywhere = pl.BlockSpec(memory_space=pl.ANY)
    return pl.pallas_call(
        pack_kernel,
        out_shape=(
            jax.ShapeDtypeStruct((groups + 1,), jnp.int32),
            jax.ShapeDtypeStruct((straight, steps - 1, rows, width), cache.dtype),
            jax.ShapeDtypeStruct((straight, rows, width), cache.dtype),
            jax.ShapeDtypeStruct((plane, steps, rows, width), cache.dtype),
        ),
        in_specs=[smem] * 9 + [pl.BlockSpec(memory_space=pltpu.VMEM), anywhere],
        out_specs=(smem,) + (anywhere,) * 3,
        scratch_shapes=[
            pltpu.VMEM((count, steps, rows, width), cache.dtype),
            pltpu.SemaphoreType.DMA((count,)),
            pltpu.SemaphoreType.DMA,
        ],
        cost_estimate=FREE,
        name="pack_pages",
    )(*scalars, fresh, cache)


def relay_kernel(me_ref, via_ref, dest_ref, got_ref, slots_ref, sem):
    plane = slots_ref.shape[0]
    count = dest_ref.shape[0]
    straight = got_ref.shape[0]
    group = me_ref[0]
    my_half = group // plane
    partner = jnp.where(group < plane, group + plane, group - plane)

    def visit(act):
        rank = jnp.int32(0)
        for j in range(count):
            target = dest_ref[j, partner]
            place = target % plane
            came = ((target // plane) == my_half) & jnp.logical_not(
                goes_via(via_ref, partner, place)
            )
            came = came & (rank < straight)

            @pl.when(came)
            def _():
                act(pltpu.make_async_copy(got_ref.at[rank], slots_ref.at[place], sem))

            rank = rank + jnp.where(came, 1, 0)

    visit(lambda copy: copy.start())
    visit(lambda copy: copy.wait())


def cost(microseconds):
    return pl.CostEstimate(flops=int(microseconds * 10**9), bytes_accessed=0, transcendentals=0)


def relay(me, via, dest, got, plane, guess):
    smem = pl.BlockSpec(memory_space=pltpu.SMEM)
    return pl.pallas_call(
        relay_kernel,
        out_shape=jax.ShapeDtypeStruct((plane,) + got.shape[1:], got.dtype),
        in_specs=[smem, smem, smem, pl.BlockSpec(memory_space=pltpu.VMEM)],
        out_specs=pl.BlockSpec(memory_space=pl.ANY),
        scratch_shapes=[pltpu.SemaphoreType.DMA],
        cost_estimate=cost(guess),
        name="relay_pages",
    )(me, via, dest, got)


def lift_kernel(me_ref, via_ref, own_ref, lifted_ref, sem):
    plane = own_ref.shape[0]
    room = lifted_ref.shape[0]
    group = me_ref[0]
    base = (group // plane) * plane
    place = group % plane

    def visit(act):
        rank = jnp.int32(0)
        for i in range(plane):
            lifted = goes_via(via_ref, base + i, place) & (rank < room)

            @pl.when(lifted)
            def _():
                act(pltpu.make_async_copy(own_ref.at[i], lifted_ref.at[rank], sem))

            rank = rank + jnp.where(lifted, 1, 0)

    visit(lambda copy: copy.start())
    visit(lambda copy: copy.wait())


def lift(me, via, own):
    smem = pl.BlockSpec(memory_space=pltpu.SMEM)
    return pl.pallas_call(
        lift_kernel,
        out_shape=jax.ShapeDtypeStruct((LIFTED,) + own.shape[1:], own.dtype),
        in_specs=[smem, smem, pl.BlockSpec(memory_space=pltpu.VMEM)],
        out_specs=pl.BlockSpec(memory_space=pl.ANY),
        scratch_shapes=[pltpu.SemaphoreType.DMA],
        cost_estimate=FREE,
        name="lift_pages",
    )(me, via, own)


def place_first_kernel(
    me_ref, via_ref, source_ref, own_ref, early_ref, lifted_ref, out_ref, rank_ref, sem
):
    plane = own_ref.shape[0]
    room = lifted_ref.shape[0]
    count, pages = out_ref.shape[:2]
    group = me_ref[0]
    my_half = group // plane
    other = (1 - my_half) * plane
    rank = jnp.int32(0)
    for i in range(plane):
        rank_ref[i] = jnp.minimum(rank, room - 1)
        rank = rank + jnp.where(goes_via(via_ref, other + i, group % plane), 1, 0)

    def visit(act):
        for j in range(count):
            source = source_ref[j]
            place = source % plane
            near = (source // plane) == my_half
            via = goes_via(via_ref, source, group % plane)
            lifted = jnp.logical_not(near) & via
            far = jnp.logical_not(near | via)

            @pl.when(near)
            def _():
                act(pltpu.make_async_copy(own_ref.at[place], out_ref.at[j], sem))

            @pl.when(far)
            def _():
                act(
                    pltpu.make_async_copy(
                        early_ref.at[place], out_ref.at[j, pl.ds(0, pages - 1)], sem
                    )
                )

            @pl.when(lifted)
            def _():
                act(pltpu.make_async_copy(lifted_ref.at[rank_ref[place]], out_ref.at[j], sem))

    visit(lambda copy: copy.start())
    visit(lambda copy: copy.wait())


def place_late_kernel(me_ref, via_ref, source_ref, late_ref, _, out_ref, sem):
    plane = late_ref.shape[0]
    count, pages = out_ref.shape[:2]
    group = me_ref[0]
    my_half = group // plane

    def visit(act):
        for j in range(count):
            source = source_ref[j]
            place = source % plane
            near = (source // plane) == my_half
            far = jnp.logical_not(near | goes_via(via_ref, source, group % plane))

            @pl.when(far)
            def _():
                act(pltpu.make_async_copy(late_ref.at[place], out_ref.at[j, pages - 1], sem))

    visit(lambda copy: copy.start())
    visit(lambda copy: copy.wait())


def place_first(me, via, sources, own, early, lifted):
    smem = pl.BlockSpec(memory_space=pltpu.SMEM)
    vmem = pl.BlockSpec(memory_space=pltpu.VMEM)
    return pl.pallas_call(
        place_first_kernel,
        out_shape=jax.ShapeDtypeStruct((sources.shape[0],) + own.shape[1:], own.dtype),
        in_specs=[smem, smem, smem, vmem, vmem, vmem],
        out_specs=pl.BlockSpec(memory_space=pltpu.HBM),
        scratch_shapes=[pltpu.SMEM((own.shape[0],), jnp.int32), pltpu.SemaphoreType.DMA],
        compiler_params=pltpu.CompilerParams(vmem_limit_bytes=ALL_VMEM),
        cost_estimate=cost(PLACE_FIRST),
        name="place_first",
    )(me, via, sources, own, early, lifted)


def place_late(me, via, sources, late, out):
    smem = pl.BlockSpec(memory_space=pltpu.SMEM)
    hbm = pl.BlockSpec(memory_space=pltpu.HBM)
    return pl.pallas_call(
        place_late_kernel,
        out_shape=jax.ShapeDtypeStruct(out.shape, out.dtype),
        in_specs=[smem, smem, smem, pl.BlockSpec(memory_space=pltpu.VMEM), hbm],
        out_specs=hbm,
        scratch_shapes=[pltpu.SemaphoreType.DMA],
        input_output_aliases={4: 0},
        compiler_params=pltpu.CompilerParams(vmem_limit_bytes=ALL_VMEM),
        cost_estimate=FREE,
        name="place_late",
    )(me, via, sources, late, out)


def local(
    queries,
    fresh_pairs,
    cache_pool,
    out_weight,
    lengths,
    page_table,
    victims,
    victim_dest,
    section_plan,
):
    steps_total = queries.shape[0]
    pool_pages, _, page_len, pair_width = cache_pool.shape[1:]
    victim_count = victims.shape[1]
    groups = lax.axis_size("grp")
    ranks = lax.axis_size("tp")
    plane = groups // HALVES
    own_group = lax.axis_index("grp")
    core = lax.axis_index("tp") % 2
    chip = lax.axis_index("tp") // 2
    fresh_steps = fresh_pairs[:, 0]
    pages = cache_pool.reshape(pool_pages, 2 * page_len, pair_width)
    dest = victim_dest.T
    table = page_table[0].T
    plan = section_plan.transpose(2, 1, 0).reshape(steps_total * victim_count, groups)
    sources = jnp.sum(
        jnp.where(dest == own_group, jnp.arange(groups)[None, :], 0), axis=1
    ).astype(jnp.int32)
    me = own_group.astype(jnp.int32)[None]
    half_groups = [list(range(h * plane, (h + 1) * plane)) for h in range(HALVES)]
    swap_halves = [(g, (g + plane) % groups) for g in range(groups)]
    swap_cores = [(r, r ^ 1) for r in range(ranks)]
    chips = ranks // 2
    crossing = (dest // plane) != (jnp.arange(groups) // plane)[None, :]
    bits = jnp.left_shift(jnp.int32(1), dest % plane)
    masks = (
        jnp.sum(jnp.where(crossing, 0, bits), axis=0),
        jnp.sum(jnp.where(crossing, bits, 0), axis=0),
        jnp.sum(crossing.astype(jnp.int32), axis=0),
    )

    def in_half(slots):
        return lax.all_to_all(slots, "grp", 0, 0, axis_index_groups=half_groups, tiled=True)

    def swap(slots):
        return lax.ppermute(slots, "grp", swap_halves)

    scalars = (me, *masks, lengths, table, victims, dest, plan)
    via, early, late, own = pack(STRAIGHT, scalars, fresh_steps, pages, plane)
    early_got = swap(early)
    own_got = in_half(own)
    kept, given = attend(
        core.astype(jnp.int32)[None],
        lengths,
        table,
        queries[:, 0],
        fresh_steps,
        pages,
        out_weight,
        ranks,
        own,
    )
    on_chip = kept + lax.ppermute(given, "tp", swap_cores)
    on_chip = on_chip.reshape(chips, -1, steps_total, on_chip.shape[1])
    late, early_got, on_chip = lax.optimization_barrier((late, early_got, on_chip))
    late_got = swap(late)
    own_share = lax.dynamic_index_in_dim(on_chip, chip, 0, keepdims=False)
    on_chip = on_chip.astype(jnp.bfloat16)
    shares = []
    for shift in range(1, chips):
        share = lax.dynamic_index_in_dim(on_chip, (chip + shift) % chips, 0, keepdims=False)
        shares.append(
            lax.ppermute(share, "tp", [(r, (r + 2 * shift) % ranks) for r in range(ranks)])
        )

    early_slots = relay(me, via, dest, early_got, plane, RELAY_FIRST)
    early_arrived = in_half(early_slots)
    lifted = lift(me, via, own_got)
    lifted_got = swap(lifted)
    late_got, _ = lax.optimization_barrier((late_got, lifted))
    migrated = place_first(me, via, sources, own_got, early_arrived, lifted_got)
    late_slots = relay(me, via, dest, late_got, plane, RELAY_LAST)
    late_arrived = in_half(late_slots)
    shares, _ = lax.optimization_barrier((shares, lifted_got))
    projected = own_share + sum(share.astype(jnp.float32) for share in shares)
    projected = projected.astype(jnp.bfloat16)
    migrated = place_late(me, via, sources, late_arrived, migrated)

    def straight_only(carry):
        no_via, early, late, own = pack(victim_count, scalars, fresh_steps, pages, plane)
        own_got = in_half(own)
        early_arrived = in_half(relay(me, no_via, dest, swap(early), plane, 0))
        late_arrived = in_half(relay(me, no_via, dest, swap(late), plane, 0))
        lifted = jnp.zeros((LIFTED,) + own.shape[1:], own.dtype)
        out = place_first(me, no_via, sources, own_got, early_arrived, lifted)
        return jnp.int32(0), place_late(me, no_via, sources, late_arrived, out)

    _, migrated = lax.while_loop(lambda c: c[0] > 0, straight_only, (via[groups], migrated))
    migrated = migrated.reshape(1, victim_count, steps_total, 2, page_len, pair_width)
    return (projected[None], migrated)


def solution(mesh):
    return jax.shard_map(
        local,
        mesh=mesh,
        in_specs=(
            P(None, "grp", None, "tp"),
            P(None, "grp", None, None, "tp"),
            P("grp", None, None, None, "tp"),
            P("tp", None),
            P("grp", None),
            P("grp", None, None),
            P("grp", None),
            P(),
            P(),
        ),
        out_specs=(P("grp", "tp", None, None), P("grp", None, None, None, None, "tp")),
        check_vma=False,
    )
```
